512 devices in a mesh: row: 32 (over x, y, core), col: 16 (over z).
Axes of the slice: x: 4, y: 4, z: 16, core: 2. Of those that a mesh axis runs over, the one named last changes fastest.
Arguments:
- front: float32 [8192, 8192], P('row', 'col'), as said below
- child_updates: bfloat16 [8192, 8192], P('row', 'col'), as said below
- block_lists: int32 [2, 16], replicated, may hold values from 0 to 31, as said below
- pivot_inverses: float32 [8, 256, 256], replicated, as said below
Outputs:
- eliminated: float32 [8192, 8192], P('row', 'col')
The draws below stay inside these ranges and needn't reach their ends.
Inputs may be any that keep to these rules, and one draw needn't show every extreme that they name: `block_lists`: row c lists the 16 different blocks of the front that child c's update blocks enter, in increasing order. `child_updates`: rows c * 4096 to (c + 1) * 4096 - 1 hold child c's update rows, its blocks in order; in them only the 256-wide column blocks named in row c of block_lists are non-zero, and the update restricted to those columns is symmetric. `front`: Symmetric. `pivot_inverses`: each of the 8 matrices is symmetric; they are given with the front and are not computed from its values.
All inputs are finite; a program needn't handle non-finite values.
Results may differ from the reference program's by a relative error of at most 0.0003.
Values may be sent and summed in bfloat16 or wider, within the bound.
A program may use at most 64 MiB of HBM per device.

```python
import jax
import jax.numpy as jnp
from jax import lax

F = 8192
B = 256
PANELS = 8
NB = 32
CB = 16


def shared_lists(key):
    chosen_rows = []
    for child_number in range(2):
        shuffled = jax.random.permutation(jax.random.fold_in(key, 101 + child_number), NB - 1).astype(jnp.int32)
        if child_number == 0:
            picked = jnp.concatenate([jnp.zeros((1,), jnp.int32), shuffled[:CB - 1] + 1])
        else:
            picked = jnp.concatenate([shuffled[:CB - 1], jnp.full((1,), NB - 1, jnp.int32)])
        chosen_rows.append(jnp.sort(picked))
    return jnp.stack(chosen_rows).astype(jnp.int32)


def symmetric_square(raw_values, scale):
    return (raw_values + jnp.swapaxes(raw_values, -1, -2)) * (scale * 0.7071067811865476)


def draw_block_lists(key, part):
    return shared_lists(key)


def draw_child_updates(key, part):
    lists_drawn = shared_lists(key)
    key = jax.random.fold_in(key, 7)
    child_rows = CB * B
    offsets = jnp.arange(B, dtype=jnp.int32)
    stacked = []
    for child_number in range(2):
        raw_values = jax.random.normal(jax.random.fold_in(key, child_number), (child_rows, child_rows), jnp.float32)
        update = symmetric_square(raw_values, 0.5)
        col_ids = (lists_drawn[child_number][:, None] * B + offsets[None, :]).reshape(-1)
        placed = jnp.zeros((child_rows, F), jnp.float32).at[:, col_ids].set(update)
        stacked.append(placed)
    return jnp.concatenate(stacked, axis=0).astype(jnp.bfloat16)


def draw_front(key, part):
    key = jax.random.fold_in(key, 11)
    raw_values = jax.random.normal(key, (F, F), jnp.float32)
    return symmetric_square(raw_values, 1.0)


def draw_pivot_inverses(key, part):
    key = jax.random.fold_in(key, 13)
    raw_values = jax.random.normal(key, (PANELS, B, B), jnp.float32)
    return symmetric_square(raw_values, 0.3 / B)


def setup_inputs(seed: int = 0) -> dict:
    splits = jax.random.split(jax.random.key(seed), 5)
    return {
        "front": draw_front(jax.random.fold_in(splits[4], 71), 0),
        "child_updates": draw_child_updates(jax.random.fold_in(splits[4], 71), 0),
        "block_lists": draw_block_lists(jax.random.fold_in(splits[4], 71), 0),
        "pivot_inverses": draw_pivot_inverses(jax.random.fold_in(splits[4], 71), 0),
    }


def reference(front, child_updates, block_lists, pivot_inverses):
    child_rows = CB * B
    offsets = jnp.arange(B, dtype=jnp.int32)
    current = front
    for child_number in range(2):
        row_ids = (block_lists[child_number][:, None] * B + offsets[None, :]).reshape(-1).astype(jnp.int32)
        rows_in = lax.slice_in_dim(child_updates, child_number * child_rows, (child_number + 1) * child_rows, axis=0).astype(jnp.float32)
        current = current.at[row_ids].add(rows_in)
    row_global = jnp.arange(F, dtype=jnp.int32)
    for number in range(PANELS):
        panel_start = number * B
        trail_start = panel_start + B
        below = (row_global >= trail_start)[:, None]
        column_part = current[:, panel_start:trail_start]
        panel_cols = jnp.where(below, column_part, jnp.zeros((), jnp.float32))
        multipliers = jnp.dot(panel_cols, pivot_inverses[number], precision=lax.Precision.HIGHEST, preferred_element_type=jnp.float32)
        update = lax.dot_general(multipliers, panel_cols, (((1,), (1,)), ((), ())), precision=lax.Precision.HIGHEST, preferred_element_type=jnp.float32)
        current = current - update
        new_part = jnp.where(below, multipliers, current[:, panel_start:trail_start])
        current = current.at[:, panel_start:trail_start].set(new_part)
    return current
```

```python
import functools

import jax
import jax.numpy as jnp
from jax import lax
from jax.experimental import pallas as pl
from jax.experimental.pallas import tpu as pltpu
from jax.sharding import PartitionSpec as P

MESH = pl.DeviceIdType.MESH
F32 = jnp.float32
BF16 = jnp.bfloat16
ZN = 16
SENDS = 48


def gather_kernel(lists, front, child, own, u_buf, t_buf, a_buf, slab, picked, routed,
                  send, recv, z_send, z_recv, t_send, t_recv, local):
    r = lax.axis_index("row")
    z = lax.axis_index("col")
    x = r // 8
    y = (r // 2) % 4
    core = r % 2
    even = core == 0
    a1 = jnp.where(even, x, y)
    a2 = jnp.where(even, y, x)

    def at(px, py, pc, pz):
        return (px * 8 + py * 2 + pc, pz)

    sibling = at(x, y, 1 - core, z)

    def along_first(step):
        moved = (a1 + step) % 4
        return at(jnp.where(even, moved, x), jnp.where(even, y, moved), core, z)

    def along_second(step):
        moved = (a2 + step) % 4
        return at(jnp.where(even, x, moved), jnp.where(even, moved, y), core, z)

    partners = [sibling]
    partners += [at((x + d) % 4, y, core, z) for d in (1, 2, 3)]
    partners += [at(x, (y + d) % 4, core, z) for d in (1, 3)]
    partners += [(r, (z + d) % ZN) for d in range(1, ZN)]
    barrier = pltpu.get_barrier_semaphore()
    for partner in partners:
        pl.semaphore_signal(barrier, inc=1, device_id=partner, device_id_type=MESH)
    pl.semaphore_wait(barrier, len(partners))

    used = [0]

    def to(src, dst, device):
        number = used[0]
        used[0] += 1
        return pltpu.make_async_remote_copy(
            src_ref=src, dst_ref=dst, send_sem=send.at[number], recv_sem=recv.at[number],
            device_id=device, device_id_type=MESH)

    def same(ref, device):
        return to(ref, ref, device)

    mine = y * 2 + core
    below = ((y + 3) % 4) * 2 + core
    above = ((y + 1) % 4) * 2 + core
    across = ((y + 2) % 4) * 2 + core
    keep = pltpu.make_async_copy(child, slab.at[mine], local.at[0])
    keep.start()
    first = [to(child, slab.at[mine], at(x, (y + 1) % 4, core, z)),
             to(child, slab.at[mine], at(x, (y + 3) % 4, core, z)),
             to(child, slab.at[mine], sibling)]
    for copy in first:
        copy.start()
    first[0].wait()
    first[1].wait()
    second = [same(slab.at[below, 0:128], at(x, (y + 1) % 4, core, z)),
              same(slab.at[above, 128:256], at(x, (y + 3) % 4, core, z)),
              same(slab.at[below], sibling),
              same(slab.at[above], sibling)]
    for copy in second:
        copy.start()
    second[0].wait()
    second[1].wait()
    third = same(slab.at[across], sibling)
    third.start()
    keep.wait()
    first[2].wait()
    second[2].wait()
    second[3].wait()
    third.wait()

    group = x // 2
    base = (x % 2) * 8

    def choice(d):
        target = ((x + d) % 4) * 8 + y * 2 + core
        place = jnp.int32(0)
        found = jnp.int32(0)
        for m in range(8):
            hit = lists[group, base + m] == target
            place = jnp.where(hit, m, place)
            found = jnp.where(hit, 1, found)
        return place, found

    for d in (2, 1, 3, 0):
        place, found = choice(d)

        @pl.loop(0, 8)
        def _(i):
            rows = pl.ds(pl.multiple_of(i * 32, 32), 32)
            block = slab[place, rows, :].astype(F32)
            picked[d, rows, :] = jnp.where(found > 0, block, 0.0).astype(BF16)

        if d == 2:
            opposite = to(picked.at[2], routed.at[2], at((x + 2) % 4, y, core, z))
            opposite.start()
        if d == 1:
            up = to(picked.at[1], routed.at[1], at((x + 1) % 4, y, core, z))
            pl.when(x < 2)(lambda: up.start())
        if d == 3:
            down = to(picked.at[3], routed.at[3], at((x + 3) % 4, y, core, z))
            pl.when(x >= 2)(lambda: down.start())
    inner = (x == 1) | (x == 2)
    opposite.wait()
    pl.when(x < 2)(lambda: up.wait_send())
    pl.when(x >= 2)(lambda: down.wait_send())

    @pl.loop(0, 8)
    def _(i):
        rows = pl.ds(pl.multiple_of(i * 32, 32), 32)
        own[rows, :] = front[rows, :] + picked[0, rows, :].astype(F32) + routed[2, rows, :].astype(F32)

    @pl.when(inner)
    def _():
        up.wait_recv()
        down.wait_recv()

        @pl.loop(0, 8)
        def _(i):
            rows = pl.ds(pl.multiple_of(i * 32, 32), 32)
            own[rows, :] = own[rows, :] + routed[1, rows, :].astype(F32) + routed[3, rows, :].astype(F32)

    def z_to(src, dst, number, pz):
        return pltpu.make_async_remote_copy(
            src_ref=src, dst_ref=dst, send_sem=z_send.at[number], recv_sem=z_recv.at[number],
            device_id=(r, pz % ZN), device_id_type=MESH)

    def z_step(s):
        back, ahead = (z - s + ZN) % ZN, (z + s) % ZN
        if s < 7:
            pair = (a_buf.at[back], a_buf.at[ahead])
        else:
            pair = (a_buf.at[back, 0:32], a_buf.at[ahead, 32:64])
        return [z_to(pair[0], pair[0], 4 + 2 * s, z + 1), z_to(pair[1], pair[1], 5 + 2 * s, z + ZN - 1)]

    def start(copies):
        for copy in copies:
            copy.start()

    def wait(copies):
        for copy in copies:
            copy.wait()

    z_scatter = [z_to(own.at[64 * q:64 * q + 64], a_buf.at[(z + 4 * q) % ZN], q, z + 4 * q) for q in (1, 2, 3)]
    z_keep = pltpu.make_async_copy(own.at[0:64], a_buf.at[z], local.at[1])

    @pl.when(z < 4)
    def _():
        start(z_scatter)
        z_keep.start()

    def u_place(px):
        return u_buf.at[core, jnp.where(even, y, px), jnp.where(even, px, y)]

    u_scatter = [to(own.at[64 * q:64 * q + 64], u_place(q), at(q, y, core, z)) for q in (1, 2, 3)]
    u_keep = pltpu.make_async_copy(own.at[0:64], u_place(0), local.at[2])

    @pl.when(x == 0)
    def _():
        start(u_scatter)
        u_keep.start()

    for q in (1, 2, 3):
        pl.when(z // 4 == q)(lambda: z_scatter[q - 1].wait_recv())
        pl.when(x == q)(lambda: u_scatter[q - 1].wait_recv())

    @pl.when(z < 4)
    def _():
        z_keep.wait()
        for copy in z_scatter:
            copy.wait_send()

    @pl.when(x == 0)
    def _():
        u_keep.wait()
        for copy in u_scatter:
            copy.wait_send()

    def plane_gather(buf, half, steps):
        left = [z_step(s) for s in steps]
        one = [same(buf.at[core, a2, a1], along_first(1)), same(buf.at[core, a2, a1], along_first(3))]
        start(one + left[0])
        wait(one)
        low, high = half
        two = [same(buf.at[core, a2, (a1 + 3) % 4, low], along_first(1)),
               same(buf.at[core, a2, (a1 + 1) % 4, high], along_first(3))]
        start(two)
        wait(left[0])
        if len(left) > 1:
            start(left[1])
        wait(two)
        three = [same(buf.at[core, a2], along_second(1)), same(buf.at[core, a2], along_second(3)),
                 same(buf.at[core, a2], sibling)]
        start(three)
        if len(left) > 1:
            wait(left[1])
        if len(left) > 2:
            start(left[2])
        wait(three[:2])
        four = [same(buf.at[core, (a2 + 3) % 4, 0:2], along_second(1)),
                same(buf.at[core, (a2 + 1) % 4, 2:4], along_second(3)),
                same(buf.at[core, (a2 + 3) % 4], sibling),
                same(buf.at[core, (a2 + 1) % 4], sibling)]
        start(four)
        if len(left) > 2:
            wait(left[2])
        if len(left) > 3:
            start(left[3])
        wait(four[:2])
        five = same(buf.at[core, (a2 + 2) % 4], sibling)
        five.start()
        if len(left) > 3:
            wait(left[3])
        wait(three[2:] + four[2:] + [five])

    plane_gather(u_buf, (pl.ds(0, 32), pl.ds(32, 32)), (0, 1, 2, 3))

    piece = core * 16 + a2 * 4 + a1
    part = piece // 8
    rows = pl.ds(pl.multiple_of((piece % 8) * 8, 8), 8)
    mid = z_step(4)
    start(mid)
    packs = []
    for k in range(7):
        slot = jnp.minimum(z * z + k, 15)
        src = u_buf.at[0, k // 2, part, rows] if k % 2 == 0 else u_buf.at[1, part, k // 2, rows]
        packs.append(pltpu.make_async_copy(src, t_buf.at[core, a2, a1, slot], local.at[3 + k]))
        pl.when((z < 4) & (2 * z >= k))(lambda: packs[k].start())
    for k in range(7):
        pl.when((z < 4) & (2 * z >= k))(lambda: packs[k].wait())

    def spread(home, d):
        ref = t_buf.at[core, a2, a1, home * home:(home + 1) * (home + 1)]
        return pltpu.make_async_remote_copy(
            src_ref=ref, dst_ref=ref, send_sem=t_send.at[d], recv_sem=t_recv.at[home],
            device_id=(r, (z + d) % ZN), device_id_type=MESH)

    for home in range(4):
        @pl.when(z == home)
        def _():
            @pl.loop(1, ZN)
            def _(d):
                spread(home, d).start()
    for home in range(4):
        pl.when(z != home)(lambda: spread(home, 1).wait_recv())
    wait(mid)
    for home in range(4):
        @pl.when(z == home)
        def _():
            @pl.loop(1, ZN)
            def _(d):
                spread(home, d).wait_send()

    plane_gather(t_buf, (pl.ds(0, 8), pl.ds(8, 8)), (5, 6, 7))


def gather(front, child, lists):
    out = (
        jax.ShapeDtypeStruct((256, 512), F32),
        jax.ShapeDtypeStruct((2, 4, 4, 64, 512), F32),
        jax.ShapeDtypeStruct((2, 4, 4, 16, 8, 512), F32),
        jax.ShapeDtypeStruct((16, 64, 512), F32),
    )
    vmem = pl.BlockSpec(memory_space=pltpu.VMEM)
    hbm = pl.BlockSpec(memory_space=pl.ANY)
    return pl.pallas_call(
        gather_kernel,
        out_shape=out,
        in_specs=[pl.BlockSpec(memory_space=pltpu.SMEM), vmem, vmem],
        out_specs=(vmem, hbm, hbm, hbm),
        scratch_shapes=[
            pltpu.VMEM((8, 256, 512), BF16),
            pltpu.VMEM((4, 256, 512), BF16),
            pltpu.VMEM((4, 256, 512), BF16),
            pltpu.SemaphoreType.DMA((SENDS,)),
            pltpu.SemaphoreType.DMA((SENDS,)),
            pltpu.SemaphoreType.DMA((20,)),
            pltpu.SemaphoreType.DMA((20,)),
            pltpu.SemaphoreType.DMA((ZN,)),
            pltpu.SemaphoreType.DMA((4,)),
            pltpu.SemaphoreType.DMA((10,)),
        ],
        compiler_params=pltpu.CompilerParams(
            collective_id=0, has_side_effects=True, vmem_limit_bytes=24 * 1024 * 1024),
    )(lists, front, child)


def parts(value):
    high = value.astype(BF16)
    return high, (value - high.astype(F32)).astype(BF16)


def product(ah, al, bh, bl):
    dot = functools.partial(jnp.dot, preferred_element_type=F32)
    return dot(ah, bh) + (dot(ah, bl) + dot(al, bh))


def eliminate_kernel(own, u_buf, t_buf, a_buf, pivots, out, xh, xl, mh, ml, acc, thin):
    r = lax.axis_index("row")
    col = lax.axis_index("col")
    columns = lax.broadcasted_iota(jnp.int32, (1, 512), 1) // 256 + 2 * col

    def subtract(j, c):
        @pl.loop(0, j)
        def _(k):
            tile = j * (j - 1) // 2 + k
            acc[...] -= product(mh[tile], ml[tile], xh[k, c], xl[k, c])

    out[...] = own[...]
    for j in range(8):
        first = (j + 1) // 2
        pivot_high, pivot_low = parts(pivots[j])

        @pl.loop(first, 4)
        def _(c):
            acc[...] = t_buf[:, c * c + j].reshape(256, 512)
            if j:
                subtract(j, c)
            xh[j, c], xl[j, c] = parts(acc[...])
            acc[...] = product(pivot_high, pivot_low, xh[j, c], xl[j, c])
            for half in range(2):
                i = 2 * c + half

                @pl.when(i > j)
                def _():
                    tile = (i * (i - 1)) // 2 + j
                    mh[tile], ml[tile] = parts(acc[:, half * 256:half * 256 + 256].T)

        acc[...] = (u_buf[0, j // 2] if j % 2 == 0 else u_buf[1, :, j // 2]).reshape(256, 512)
        if j:
            subtract(j, 4)
        acc[...] = jnp.where(columns > j, acc[...], 0.0)
        xh[j, 4], xl[j, 4] = parts(acc[...])

        side = slice((j % 2) * 256, (j % 2) * 256 + 256)
        thin[...] = a_buf[:, j // 2, :, side].reshape(256, 256)
        if j:
            @pl.loop(0, j)
            def _(k):
                thin[...] -= product(mh[28 + k], ml[28 + k], xh[k, j // 2, :, side], xl[k, j // 2, :, side])
        panel = jnp.where(r > j, thin[...], 0.0)
        panel_high, panel_low = parts(panel)
        thin[...] = product(panel_high, panel_low, pivot_high, pivot_low)
        mh[28 + j], ml[28 + j] = parts(thin[...])
        out[...] -= product(mh[28 + j], ml[28 + j], xh[j, 4], xl[j, 4])

        @pl.when((col == j // 2) & (r > j))
        def _():
            out[:, side] = thin[...]


def eliminate(own, u_buf, t_buf, a_buf, pivots):
    vmem = pl.BlockSpec(memory_space=pltpu.VMEM)
    return pl.pallas_call(
        eliminate_kernel,
        out_shape=jax.ShapeDtypeStruct((256, 512), F32),
        in_specs=[vmem] * 5,
        out_specs=vmem,
        scratch_shapes=[
            pltpu.VMEM((8, 5, 256, 512), BF16),
            pltpu.VMEM((8, 5, 256, 512), BF16),
            pltpu.VMEM((36, 256, 256), BF16),
            pltpu.VMEM((36, 256, 256), BF16),
            pltpu.VMEM((256, 512), F32),
            pltpu.VMEM((256, 256), F32),
        ],
        compiler_params=pltpu.CompilerParams(vmem_limit_bytes=56 * 1024 * 1024),
    )(own, u_buf, t_buf.reshape(32, 16, 8, 512), a_buf.reshape(4, 4, 64, 512), pivots)


def on_device(front, child_updates, block_lists, pivot_inverses):
    own, u_buf, t_buf, a_buf = gather(front, child_updates, block_lists)
    return eliminate(own, u_buf, t_buf, a_buf, pivot_inverses)


def solution(mesh):
    return jax.shard_map(
        on_device,
        mesh=mesh,
        in_specs=(P("row", "col"), P("row", "col"), P(), P()),
        out_specs=P("row", "col"),
        check_vma=False,
    )
```

```python
import functools

import jax
import jax.numpy as jnp
from jax import lax
from jax.experimental import pallas as pl
from jax.experimental.pallas import tpu as pltpu
from jax.sharding import PartitionSpec as P

MESH = pl.DeviceIdType.MESH
F32 = jnp.float32
BF16 = jnp.bfloat16
ZN = 16
RN = 32


def start(copies):
    for copy in copies:
        copy.start()


def wait(copies):
    for copy in copies:
        copy.wait()


def parts(value):
    high = value.astype(BF16)
    return high, (value - high.astype(F32)).astype(BF16)


def product(ah, al, bh, bl):
    dot = functools.partial(jnp.dot, preferred_element_type=F32)
    return dot(ah, bh) + (dot(ah, bl) + dot(al, bh))


def front_kernel(lists, front, child, pivots, out, own, u_buf, t_buf, a_buf, slab_low, slab_high, picked, routed,
                 wh, wl, xh, xl, mh, ml, flat, send, recv, z_send, z_recv, t_send, t_recv, local):
    r = lax.axis_index("row")
    z = lax.axis_index("col")
    x = r // 8
    y = (r // 2) % 4
    core = r % 2
    even = core == 0
    a1 = jnp.where(even, x, y)
    a2 = jnp.where(even, y, x)

    def at(px, py, pc):
        return (px * 8 + py * 2 + pc, z)

    sibling = at(x, y, 1 - core)

    def along_first(step):
        moved = (a1 + step) % 4
        return at(jnp.where(even, moved, x), jnp.where(even, y, moved), core)

    def along_second(step):
        moved = (a2 + step) % 4
        return at(jnp.where(even, x, moved), jnp.where(even, moved, y), core)

    barrier = pltpu.get_barrier_semaphore()

    @pl.loop(1, RN)
    def _(d):
        pl.semaphore_signal(barrier, inc=1, device_id=((r + d) % RN, z), device_id_type=MESH)

    @pl.loop(1, ZN)
    def _(d):
        pl.semaphore_signal(barrier, inc=1, device_id=(r, (z + d) % ZN), device_id_type=MESH)

    pl.semaphore_wait(barrier, RN + ZN - 2)

    used = [0]

    def to(src, dst, device):
        number = used[0]
        used[0] += 1
        return pltpu.make_async_remote_copy(
            src_ref=src, dst_ref=dst, send_sem=send.at[number], recv_sem=recv.at[number],
            device_id=device, device_id_type=MESH)

    def same(ref, device):
        return to(ref, ref, device)

    halves = [pl.ds(0, 128), pl.ds(128, 128)]
    slabs = [slab_low, slab_high]
    place_of = [((y + d) % 4) * 2 + core for d in range(4)]
    keep, first, passed = [], [], []
    for h, rows in enumerate(halves):
        slab = slabs[h]
        keep.append(pltpu.make_async_copy(child.at[rows], slab.at[place_of[0]], local.at[h]))
        first.append([to(child.at[rows], slab.at[place_of[0]], at(x, (y + d) % 4, core)) for d in (1, 3, 2)]
                     + [to(child.at[rows], slab.at[place_of[0]], sibling)])
        passed.append([same(slab.at[place_of[d]], sibling) for d in (1, 3, 2)])
    for h in range(2):
        start(first[h] + [keep[h]])

    group = x // 2
    base = (x % 2) * 8

    def choice(d):
        target = ((x + d) % 4) * 8 + y * 2 + core
        place = jnp.int32(0)
        found = jnp.int32(0)
        for m in range(8):
            hit = lists[group, base + m] == target
            place = jnp.where(hit, m, place)
            found = jnp.where(hit, 1, found)
        return place, found

    choices = [choice(d) for d in range(4)]
    up, opposite, down = [], [], []
    for h, rows in enumerate(halves):
        up.append(to(picked.at[1, rows], routed.at[1, rows], at((x + 1) % 4, y, core)))
        opposite.append(to(picked.at[2, rows], routed.at[2, rows], at((x + 2) % 4, y, core)))
        down.append(to(picked.at[3, rows], routed.at[3, rows], at((x + 3) % 4, y, core)))
    for h in range(2):
        wait(first[h][:3])
        start(passed[h])
        keep[h].wait()
        first[h][3].wait()
        wait(passed[h])
        for d in (2, 1, 3, 0):
            place, found = choices[d]

            @pl.loop(0, 4)
            def _(i):
                rows = pl.ds(pl.multiple_of(h * 128 + i * 32, 32), 32)
                block = slabs[h][place, pl.ds(pl.multiple_of(i * 32, 32), 32), :].astype(F32)
                picked[d, rows, :] = jnp.where(found > 0, block, 0.0).astype(BF16)

            if d == 2:
                opposite[h].start()
            if d == 1:
                pl.when(x < 2)(lambda: up[h].start())
            if d == 3:
                pl.when(x >= 2)(lambda: down[h].start())
    inner = (x == 1) | (x == 2)
    for h in range(2):
        opposite[h].wait()
        pl.when(x < 2)(lambda: up[h].wait_send())
        pl.when(x >= 2)(lambda: down[h].wait_send())

        @pl.loop(0, 4)
        def _(i):
            rows = pl.ds(pl.multiple_of(h * 128 + i * 32, 32), 32)
            own[rows, :] = front[rows, :] + picked[0, rows, :].astype(F32) + routed[2, rows, :].astype(F32)

        @pl.when(inner)
        def _():
            up[h].wait_recv()
            down[h].wait_recv()

            @pl.loop(0, 4)
            def _(i):
                rows = pl.ds(pl.multiple_of(h * 128 + i * 32, 32), 32)
                own[rows, :] = own[rows, :] + routed[1, rows, :].astype(F32) + routed[3, rows, :].astype(F32)

    def u_place(px):
        return u_buf.at[core, jnp.where(even, y, px), jnp.where(even, px, y)]

    u_scatter = [to(own.at[64 * q:64 * q + 64], u_place(q), at(q, y, core)) for q in (1, 2, 3)]
    u_keep = pltpu.make_async_copy(own.at[0:64], u_place(0), local.at[2])

    @pl.when(x == 0)
    def _():
        start(u_scatter)
        u_keep.start()

    row_block = y * 2 + core
    piece = core * 16 + a2 * 4 + a1
    t_slot = jnp.minimum(z * z + row_block, 15)

    def t_copy(p):
        pc, p2, p1 = p // 16, (p // 4) % 4, p % 4
        px, py = jnp.where(pc == 0, p1, p2), jnp.where(pc == 0, p2, p1)
        return pltpu.make_async_remote_copy(
            src_ref=own.at[pl.ds(pl.multiple_of(p * 8, 8), 8)], dst_ref=t_buf.at[pc, p2, p1, t_slot],
            send_sem=t_send.at[p], recv_sem=t_recv.at[row_block],
            device_id=at(px, py, pc), device_id_type=MESH)

    t_keep = pltpu.make_async_copy(
        own.at[pl.ds(pl.multiple_of(piece * 8, 8), 8)], t_buf.at[core, a2, a1, t_slot], local.at[3])
    t_source = (x == 0) & (z < 4) & (row_block <= 2 * z)

    @pl.when(t_source)
    def _():
        t_keep.start()

        @pl.loop(1, RN)
        def _(d):
            t_copy((piece + d) % RN).start()

    def plane_first(ref):
        return [same(ref(core, a2, a1), along_first(d)) for d in (1, 3, 2)]

    def plane_second(ref):
        return [same(ref(core, a2, slice(0, 4)), along_second(d)) for d in (1, 3)] + [
            same(ref(core, a2, slice(0, 4)), sibling)]

    def plane_third(ref):
        return [same(ref(core, (a2 + 3) % 4, slice(0, 2)), along_second(1)),
                same(ref(core, (a2 + 1) % 4, slice(2, 4)), along_second(3)),
                same(ref(core, (a2 + 3) % 4, slice(0, 4)), sibling),
                same(ref(core, (a2 + 1) % 4, slice(0, 4)), sibling)]

    def plane_last(ref):
        return [same(ref(core, (a2 + 2) % 4, slice(0, 4)), sibling)]

    def plane_gather(ref):
        return plane_first(ref), plane_second(ref), plane_third(ref), plane_last(ref)

    u_one, u_two, u_three, u_four = plane_gather(lambda *place: u_buf.at[place])
    for q in (1, 2, 3):
        pl.when(x == q)(lambda: u_scatter[q - 1].wait_recv())
    pl.when(x == 0)(lambda: u_keep.wait())
    start(u_one)

    for k in range(7):
        source_here = (x == 0) & (row_block == k)

        @pl.when((z < 4) & (2 * z >= k))
        def _():
            slot = jnp.minimum(z * z + k, 15)
            arrived = t_buf.at[core, a2, a1, slot]
            copy = pltpu.make_async_remote_copy(
                src_ref=arrived, dst_ref=arrived, send_sem=t_send.at[0], recv_sem=t_recv.at[k],
                device_id=sibling, device_id_type=MESH)
            pl.when(source_here)(lambda: t_keep.wait())
            pl.when(jnp.logical_not(source_here))(lambda: copy.wait_recv())

    homes = [t_buf.at[core, a2, a1, home * home:(home + 1) * (home + 1)] for home in range(4)]

    def z_copy(ref, send_number, recv_number, pz):
        return pltpu.make_async_remote_copy(
            src_ref=ref, dst_ref=ref, send_sem=z_send.at[send_number], recv_sem=z_recv.at[recv_number],
            device_id=(r, pz % ZN), device_id_type=MESH)

    far = [[z_copy(homes[home], d, home, z + 4 * d) for d in (1, 2, 3)] for home in range(4)]
    near = [[z_copy(homes[home], 3 + d, 4 + home, (z // 4) * 4 + (z + d) % 4) for d in (1, 2, 3)]
            for home in range(4)]
    for home in range(4):
        pl.when(z == home)(lambda: start(far[home]))
    wait(u_one)
    start(u_two)
    for home in range(4):
        pl.when((z >= 4) & (z % 4 == home))(lambda: far[home][0].wait_recv())
        pl.when(z % 4 == home)(lambda: start(near[home]))

    def a_copy(src, dst, number, pz):
        return pltpu.make_async_remote_copy(
            src_ref=src, dst_ref=dst, send_sem=z_send.at[number], recv_sem=z_recv.at[number],
            device_id=(r, pz % ZN), device_id_type=MESH)

    a_scatter = [a_copy(own.at[64 * q:64 * q + 64], a_buf.at[(z + 4 * q) % ZN], 8 + q, z + 4 * q)
                 for q in (1, 2, 3)]
    a_keep = pltpu.make_async_copy(own.at[0:64], a_buf.at[z], local.at[4])

    @pl.when(z < 4)
    def _():
        start(a_scatter)
        a_keep.start()

    def a_step(s):
        back, ahead = a_buf.at[(z - s + ZN) % ZN], a_buf.at[(z + s) % ZN]
        if s == 7:
            back, ahead = a_buf.at[(z + 9) % ZN, 0:32], a_buf.at[(z + 7) % ZN, 32:64]
        return [a_copy(back, back, 12 + 2 * s, z + 1), a_copy(ahead, ahead, 13 + 2 * s, z + ZN - 1)]

    ring = [a_step(s) for s in range(8)]
    turn = [0]

    def advance():
        s = turn[0]
        turn[0] += 1
        if s == 0:
            for q in (1, 2, 3):
                pl.when(z // 4 == q)(lambda: a_scatter[q - 1].wait_recv())
            pl.when(z < 4)(lambda: a_keep.wait())
        elif s <= 8:
            wait(ring[s - 1])
        if s < 8:
            start(ring[s])

    wait(u_two[:2])
    start(u_three)
    for home in range(4):
        pl.when(z % 4 != home)(lambda: near[home][0].wait_recv())
    wide = plane_gather(lambda *place: t_buf.at[place + (slice(0, 9),)])
    narrow = plane_gather(lambda *place: t_buf.at[place + (slice(9, 16),)])
    start(wide[0])
    start(narrow[0])
    wait(u_three[:2])
    start(u_four)
    wait(wide[0])
    start(wide[1])
    wait(narrow[0])
    start(narrow[1])
    wait(u_two[2:] + u_three[2:] + u_four)
    wait(wide[1][:2])
    start(wide[2])
    advance()
    wait(narrow[1][:2])
    start(narrow[2])
    advance()
    wait(wide[2][:2])
    start(wide[3])
    advance()
    wait(wide[1][2:] + wide[2][2:] + wide[3])

    columns = lax.broadcasted_iota(jnp.int32, (1, 512), 1) // 256 + 2 * z
    blocks = [pl.ds(256 * j, 256) for j in range(8)]

    def lead(j, c):
        n = 256 * j
        me, cols = blocks[j], pl.ds(512 * c, 512)
        value = t_buf[:, :, :, c * c + j].reshape(256, 512)
        if j:
            value = value - product(wh[me, 0:n], wl[me, 0:n], wh[0:n, cols], wl[0:n, cols])
        high, low = parts(value)
        wh[me, cols] = high
        wl[me, cols] = low
        pivot_high, pivot_low = parts(pivots[j])
        scaled = product(pivot_high, pivot_low, high, low)
        for half in range(2):
            i = 2 * c + half
            if i > j:
                wh[blocks[i], me], wl[blocks[i], me] = parts(scaled[:, half * 256:half * 256 + 256].T)

    def plane_row(j):
        n = 256 * j
        me = blocks[j]
        value = (u_buf[0, j // 2] if j % 2 == 0 else u_buf[1, :, j // 2]).reshape(256, 512)
        if j:
            value = value - product(wh[me, 0:n], wl[me, 0:n], xh[0:n], xl[0:n])
        xh[me], xl[me] = parts(jnp.where(columns > j, value, 0.0))

    for j in range(6):
        for c in range((j + 1) // 2, 3):
            lead(j, c)
        plane_row(j)
        if j == 2:
            wait(narrow[2][:2])
            start(narrow[3])
        if j in (1, 3, 5):
            advance()
    wait(narrow[1][2:] + narrow[2][2:] + narrow[3])
    for j in range(7):
        lead(j, 3)
        if j in (3, 6):
            advance()
    plane_row(6)
    plane_row(7)
    advance()
    for j in range(8):
        if j == 0:
            while turn[0] <= 8:
                advance()
        n = 256 * j
        me = blocks[j]
        side = slice((j % 2) * 256, (j % 2) * 256 + 256)
        panel = jnp.concatenate([a_buf[4 * q + j // 2, :, side] for q in range(4)], axis=0)
        if j:
            panel = panel - product(mh[:, 0:n], ml[:, 0:n], wh[0:n, me], wl[0:n, me])
        high, low = parts(jnp.where(r > j, panel, 0.0))
        pivot_high, pivot_low = parts(pivots[j])
        flat[j] = product(high, low, pivot_high, pivot_low)
        mh[:, me], ml[:, me] = parts(flat[j])
    out[...] = own[...] - product(mh[...], ml[...], xh[...], xl[...])
    for j in range(8):
        @pl.when((z == j // 2) & (r > j))
        def _():
            out[:, (j % 2) * 256:(j % 2) * 256 + 256] = flat[j]

    @pl.when(x == 0)
    def _():
        for copy in u_scatter:
            copy.wait_send()

    @pl.when(t_source)
    def _():
        @pl.loop(1, RN)
        def _(d):
            t_copy((piece + d) % RN).wait_send()

    @pl.when(z < 4)
    def _():
        for copy in a_scatter:
            copy.wait_send()

    for home in range(4):
        @pl.when(z == home)
        def _():
            for copy in far[home]:
                copy.wait_send()

        @pl.when(z % 4 == home)
        def _():
            for copy in near[home]:
                copy.wait_send()


def on_device(front, child_updates, block_lists, pivot_inverses):
    vmem = pl.BlockSpec(memory_space=pltpu.VMEM)
    return pl.pallas_call(
        front_kernel,
        out_shape=jax.ShapeDtypeStruct((256, 512), F32),
        in_specs=[pl.BlockSpec(memory_space=pltpu.SMEM), vmem, vmem, vmem],
        out_specs=vmem,
        scratch_shapes=[
            pltpu.VMEM((256, 512), F32),
            pltpu.VMEM((2, 4, 4, 64, 512), F32),
            pltpu.VMEM((2, 4, 4, 16, 8, 512), F32),
            pltpu.VMEM((16, 64, 512), F32),
            pltpu.VMEM((8, 128, 512), BF16),
            pltpu.VMEM((8, 128, 512), BF16),
            pltpu.VMEM((4, 256, 512), BF16),
            pltpu.VMEM((4, 256, 512), BF16),
            pltpu.VMEM((2048, 2048), BF16),
            pltpu.VMEM((2048, 2048), BF16),
            pltpu.VMEM((2048, 512), BF16),
            pltpu.VMEM((2048, 512), BF16),
            pltpu.VMEM((256, 2048), BF16),
            pltpu.VMEM((256, 2048), BF16),
            pltpu.VMEM((8, 256, 256), F32),
            pltpu.SemaphoreType.DMA((72,)),
            pltpu.SemaphoreType.DMA((72,)),
            pltpu.SemaphoreType.DMA((28,)),
            pltpu.SemaphoreType.DMA((28,)),
            pltpu.SemaphoreType.DMA((RN,)),
            pltpu.SemaphoreType.DMA((8,)),
            pltpu.SemaphoreType.DMA((8,)),
        ],
        compiler_params=pltpu.CompilerParams(
            collective_id=0, has_side_effects=True, vmem_limit_bytes=60 * 1024 * 1024),
    )(block_lists, front, child_updates, pivot_inverses)


def solution(mesh):
    return jax.shard_map(
        on_device,
        mesh=mesh,
        in_specs=(P("row", "col"), P("row", "col"), P(), P()),
        out_specs=P("row", "col"),
        check_vma=False,
    )
```

```python
import functools

import jax
import jax.numpy as jnp
from jax import lax
from jax.experimental import pallas as pl
from jax.experimental.pallas import tpu as pltpu
from jax.sharding import PartitionSpec as P

MESH = pl.DeviceIdType.MESH
F32 = jnp.float32
BF16 = jnp.bfloat16
ZN = 16
RN = 32


def start(copies):
    for copy in copies:
        copy.start()


def wait(copies):
    for copy in copies:
        copy.wait()


def parts(value):
    high = value.astype(BF16)
    return high, (value - high.astype(F32)).astype(BF16)


def product(ah, al, bh, bl):
    dot = functools.partial(jnp.dot, preferred_element_type=F32)
    return dot(ah, bh) + (dot(ah, bl) + dot(al, bh))


def front_kernel(lists, front_hbm, child, pivots_hbm, out, front, pivots, own, u_buf, t_buf, a_buf, slab_low, slab_high, picked, routed,
                 wh, wl, xh, xl, mh, ml, flat, send, recv, z_send, z_recv, t_send, t_recv, local):
    r = lax.axis_index("row")
    z = lax.axis_index("col")
    x = r // 8
    y = (r // 2) % 4
    core = r % 2
    even = core == 0
    a1 = jnp.where(even, x, y)
    a2 = jnp.where(even, y, x)

    def at(px, py, pc):
        return (px * 8 + py * 2 + pc, z)

    sibling = at(x, y, 1 - core)

    def along_first(step):
        moved = (a1 + step) % 4
        return at(jnp.where(even, moved, x), jnp.where(even, y, moved), core)

    def along_second(step):
        moved = (a2 + step) % 4
        return at(jnp.where(even, x, moved), jnp.where(even, moved, y), core)

    front_in = pltpu.make_async_copy(front_hbm, front, local.at[5])
    pivots_in = pltpu.make_async_copy(pivots_hbm, pivots, local.at[6])
    front_in.start()
    pivots_in.start()

    group_z = (z // 4) * 4
    partners = [sibling]
    partners += [at((x + d) % 4, y, core) for d in (1, 2, 3)]
    partners += [at(x, (y + d) % 4, core) for d in (1, 2, 3)]
    partners += [(r, (z + d) % ZN) for d in (1, 4, 8, 12, 15)]
    partners += [(r, group_z + (z + d) % 4) for d in (1, 2, 3)]
    barrier = pltpu.get_barrier_semaphore()
    for partner in partners:
        pl.semaphore_signal(barrier, inc=1, device_id=partner, device_id_type=MESH)

    @pl.when(z < 4)
    def _():
        for k in range(8):
            @pl.when(r != k)
            def _():
                pl.semaphore_signal(barrier, inc=1, device_id=(k, z), device_id_type=MESH)

    pl.semaphore_wait(barrier, len(partners) + jnp.where((x == 0) & (z < 4), RN - 1, 0))

    used = [0]

    def to(src, dst, device):
        number = used[0]
        used[0] += 1
        return pltpu.make_async_remote_copy(
            src_ref=src, dst_ref=dst, send_sem=send.at[number], recv_sem=recv.at[number],
            device_id=device, device_id_type=MESH)

    def same(ref, device):
        return to(ref, ref, device)

    halves = [pl.ds(0, 128), pl.ds(128, 128)]
    slabs = [slab_low, slab_high]
    place_of = [((y + d) % 4) * 2 + core for d in range(4)]
    keep, first, passed = [], [], []
    for h, rows in enumerate(halves):
        slab = slabs[h]
        keep.append(pltpu.make_async_copy(child.at[rows], slab.at[place_of[0]], local.at[h]))
        first.append([to(child.at[rows], slab.at[place_of[0]], at(x, (y + d) % 4, core)) for d in (1, 3, 2)]
                     + [to(child.at[rows], slab.at[place_of[0]], sibling)])
        passed.append([same(slab.at[place_of[d]], sibling) for d in (1, 3, 2)])
    for h in range(2):
        start(first[h] + [keep[h]])

    group = x // 2
    base = (x % 2) * 8

    def choice(d):
        target = ((x + d) % 4) * 8 + y * 2 + core
        place = jnp.int32(0)
        found = jnp.int32(0)
        for m in range(8):
            hit = lists[group, base + m] == target
            place = jnp.where(hit, m, place)
            found = jnp.where(hit, 1, found)
        return place, found

    choices = [choice(d) for d in range(4)]
    up, opposite, down = [], [], []
    for h, rows in enumerate(halves):
        up.append(to(picked.at[1, rows], routed.at[1, rows], at((x + 1) % 4, y, core)))
        opposite.append(to(picked.at[2, rows], routed.at[2, rows], at((x + 2) % 4, y, core)))
        down.append(to(picked.at[3, rows], routed.at[3, rows], at((x + 3) % 4, y, core)))
    def pick(h, d):
        place, found = choices[d]

        @pl.loop(0, 4)
        def _(i):
            block = slabs[h][place, pl.ds(pl.multiple_of(i * 32, 32), 32), :].astype(F32)
            rows = pl.ds(pl.multiple_of(h * 128 + i * 32, 32), 32)
            picked[d, rows, :] = jnp.where(found > 0, block, 0.0).astype(BF16)

    for h in range(2):
        wait(first[h][:3])
        start(passed[h])
        keep[h].wait()
        first[h][3].wait()
        wait(passed[h])
        pick(h, 2)
        opposite[h].start()
    for h in range(2):
        pick(h, 1)
        pl.when(x < 2)(lambda: up[h].start())
        pick(h, 3)
        pl.when(x >= 2)(lambda: down[h].start())
        pick(h, 0)
    front_in.wait()
    for h in range(2):
        opposite[h].wait()

        @pl.loop(0, 4)
        def _(i):
            rows = pl.ds(pl.multiple_of(h * 128 + i * 32, 32), 32)
            own[rows, :] = front[rows, :] + picked[0, rows, :].astype(F32) + routed[2, rows, :].astype(F32)

    def u_place(px):
        return u_buf.at[core, jnp.where(even, y, px), jnp.where(even, px, y)]

    u_scatter = [to(own.at[64 * q:64 * q + 64], u_place(q), at(q, y, core)) for q in (1, 2, 3)]
    u_keep = pltpu.make_async_copy(own.at[0:64], u_place(0), local.at[2])

    @pl.when(x == 0)
    def _():
        start(u_scatter)
        u_keep.start()

    row_block = y * 2 + core
    piece = core * 16 + a2 * 4 + a1
    t_slot = jnp.minimum(z * z + row_block, 15)

    def t_copy(p):
        pc, p2, p1 = p // 16, (p // 4) % 4, p % 4
        px, py = jnp.where(pc == 0, p1, p2), jnp.where(pc == 0, p2, p1)
        return pltpu.make_async_remote_copy(
            src_ref=own.at[pl.ds(pl.multiple_of(p * 8, 8), 8)], dst_ref=t_buf.at[pc, p2, p1, t_slot],
            send_sem=t_send.at[p], recv_sem=t_recv.at[row_block],
            device_id=at(px, py, pc), device_id_type=MESH)

    t_keep = pltpu.make_async_copy(
        own.at[pl.ds(pl.multiple_of(piece * 8, 8), 8)], t_buf.at[core, a2, a1, t_slot], local.at[3])
    t_source = (x == 0) & (z < 4) & (row_block <= 2 * z)

    @pl.when(t_source)
    def _():
        t_keep.start()

        @pl.loop(1, RN)
        def _(d):
            t_copy((piece + d) % RN).start()

    def plane_first(ref):
        return [same(ref(core, a2, a1), along_first(d)) for d in (1, 3, 2)]

    def plane_second(ref):
        return [same(ref(core, a2, slice(0, 4)), along_second(d)) for d in (1, 3)] + [
            same(ref(core, a2, slice(0, 4)), sibling)]

    def plane_third(ref):
        return [same(ref(core, (a2 + 3) % 4, slice(0, 2)), along_second(1)),
                same(ref(core, (a2 + 1) % 4, slice(2, 4)), along_second(3)),
                same(ref(core, (a2 + 3) % 4, slice(0, 4)), sibling),
                same(ref(core, (a2 + 1) % 4, slice(0, 4)), sibling)]

    def plane_last(ref):
        return [same(ref(core, (a2 + 2) % 4, slice(0, 4)), sibling)]

    def plane_gather(ref):
        return plane_first(ref), plane_second(ref), plane_third(ref), plane_last(ref)

    u_one, u_two, u_three, u_four = plane_gather(lambda *place: u_buf.at[place])
    for q in (1, 2, 3):
        pl.when(x == q)(lambda: u_scatter[q - 1].wait_recv())
    pl.when(x == 0)(lambda: u_keep.wait())
    start(u_one)

    for k in range(7):
        source_here = (x == 0) & (row_block == k)

        @pl.when((z < 4) & (2 * z >= k))
        def _():
            slot = jnp.minimum(z * z + k, 15)
            arrived = t_buf.at[core, a2, a1, slot]
            copy = pltpu.make_async_remote_copy(
                src_ref=arrived, dst_ref=arrived, send_sem=t_send.at[0], recv_sem=t_recv.at[k],
                device_id=sibling, device_id_type=MESH)
            pl.when(source_here)(lambda: t_keep.wait())
            pl.when(jnp.logical_not(source_here))(lambda: copy.wait_recv())

    homes = [t_buf.at[core, a2, a1, home * home:(home + 1) * (home + 1)] for home in range(4)]

    def z_copy(src, dst, number, arrival, pz):
        return pltpu.make_async_remote_copy(
            src_ref=src, dst_ref=dst, send_sem=z_send.at[number], recv_sem=z_recv.at[arrival],
            device_id=(r, pz % ZN), device_id_type=MESH)

    far = [[z_copy(homes[home], homes[home], d, home, z + 4 * d) for d in (1, 2, 3)] for home in range(4)]
    near = [[z_copy(homes[home], homes[home], 3 + d, 4 + home, group_z + (z + d) % 4) for d in (1, 2, 3)]
            for home in range(4)]
    for home in range(4):
        pl.when(z == home)(lambda: start(far[home]))

    inner = (x == 1) | (x == 2)
    for h in range(2):
        pl.when(x < 2)(lambda: up[h].wait_send())
        pl.when(x >= 2)(lambda: down[h].wait_send())

        @pl.when(inner)
        def _():
            up[h].wait_recv()
            down[h].wait_recv()

            @pl.loop(0, 4)
            def _(i):
                rows = pl.ds(pl.multiple_of(h * 128 + i * 32, 32), 32)
                own[rows, :] = own[rows, :] + routed[1, rows, :].astype(F32) + routed[3, rows, :].astype(F32)

    a_scatter = [z_copy(own.at[64 * q:64 * q + 64], a_buf.at[(z + 4 * q) % ZN], 8 + q, 8 + q, z + 4 * q)
                 for q in (1, 2, 3)]
    a_keep = pltpu.make_async_copy(own.at[0:64], a_buf.at[z], local.at[4])

    @pl.when(z < 4)
    def _():
        a_scatter[1].start()
        a_keep.start()

    def a_step(s, half):
        rows = slice(32 * half, 32 * half + 32)
        back, ahead = a_buf.at[(z + ZN - s) % ZN, rows], a_buf.at[(z + s) % ZN, rows]
        number = 12 + 4 * s + 2 * half
        pair = [z_copy(back, back, number, number, z + 1), z_copy(ahead, ahead, number + 1, number + 1, z + ZN - 1)]
        return pair if s < 7 else pair[half:half + 1]

    ring = [a_step(s, half) for s in range(8) for half in range(2)]
    turn = [0]

    def advance(count=1):
        for _ in range(count):
            event = turn[0]
            turn[0] += 1
            if event == 0:
                for q in (1, 2, 3):
                    pl.when(z // 4 == q)(lambda: a_scatter[q - 1].wait_recv())
                pl.when(z < 4)(lambda: a_keep.wait())
                start(ring[0] + ring[1])
            elif event <= 16:
                wait(ring[event - 1])
                if event + 1 < 16:
                    start(ring[event + 1])

    wait(u_one)
    start(u_two)
    for home in range(4):
        pl.when((z >= 4) & (z % 4 == home))(lambda: far[home][0].wait_recv())
        pl.when(z % 4 == home)(lambda: start(near[home]))

    @pl.when(z < 4)
    def _():
        a_scatter[0].start()
        a_scatter[2].start()

    wide = plane_gather(lambda *place: t_buf.at[place + (slice(0, 9),)])
    narrow = plane_gather(lambda *place: t_buf.at[place + (slice(9, 16),)])
    wait(u_two[:2])
    start(u_three)
    for home in range(3):
        pl.when(z % 4 != home)(lambda: near[home][0].wait_recv())
    start(wide[0])
    wait(u_three[:2])
    start(u_four)
    wait(wide[0])
    start(wide[1])
    pl.when(z % 4 != 3)(lambda: near[3][0].wait_recv())
    start(narrow[0])
    advance(2)
    wait(narrow[0])
    start(narrow[1])
    advance(2)
    wait(u_two[2:] + u_three[2:] + u_four)
    wait(wide[1][:2])
    start(wide[2])
    advance(2)
    wait(narrow[1][:2])
    start(narrow[2])
    advance(2)
    wait(wide[2][:2])
    start(wide[3])
    pivots_in.wait()
    advance(1)
    wait(wide[1][2:] + wide[2][2:] + wide[3])

    columns = lax.broadcasted_iota(jnp.int32, (1, 512), 1) // 256 + 2 * z
    blocks = [pl.ds(256 * j, 256) for j in range(8)]

    def lead(j, c):
        n = 256 * j
        me, cols = blocks[j], pl.ds(512 * c, 512)
        value = t_buf[:, :, :, c * c + j].reshape(256, 512)
        if j:
            value = value - product(wh[me, 0:n], wl[me, 0:n], wh[0:n, cols], wl[0:n, cols])
        high, low = parts(value)
        wh[me, cols] = high
        wl[me, cols] = low
        pivot_high, pivot_low = parts(pivots[j])
        scaled = product(pivot_high, pivot_low, high, low)
        for half in range(2):
            i = 2 * c + half
            if i > j:
                wh[blocks[i], me], wl[blocks[i], me] = parts(scaled[:, half * 256:half * 256 + 256].T)

    def plane_row(j):
        n = 256 * j
        me = blocks[j]
        value = (u_buf[0, j // 2] if j % 2 == 0 else u_buf[1, :, j // 2]).reshape(256, 512)
        if j:
            value = value - product(wh[me, 0:n], wl[me, 0:n], xh[0:n], xl[0:n])
        xh[me], xl[me] = parts(jnp.where(columns > j, value, 0.0))

    def panel_step(j):
        n = 256 * j
        me = blocks[j]
        side = slice((j % 2) * 256, (j % 2) * 256 + 256)
        panel = jnp.concatenate([a_buf[4 * q + j // 2, :, side] for q in range(4)], axis=0)
        if j:
            panel = panel - product(mh[:, 0:n], ml[:, 0:n], wh[0:n, me], wl[0:n, me])
        high, low = parts(jnp.where(r > j, panel, 0.0))
        pivot_high, pivot_low = parts(pivots[j])
        flat[j] = product(high, low, pivot_high, pivot_low)
        mh[:, me], ml[:, me] = parts(flat[j])

    for j in range(6):
        for c in range((j + 1) // 2, 3):
            lead(j, c)
        plane_row(j)
        if j == 1:
            wait(narrow[2][:2])
            start(narrow[3])
        advance()
    wait(narrow[1][2:] + narrow[2][2:] + narrow[3])
    lead(0, 3)
    advance()
    lead(1, 3)
    advance()
    assert turn[0] == 17
    for j in range(7):
        if j > 1:
            lead(j, 3)
        panel_step(j)
    plane_row(6)
    plane_row(7)
    panel_step(7)
    out[...] = own[...] - product(mh[...], ml[...], xh[...], xl[...])
    for j in range(8):
        @pl.when((z == j // 2) & (r > j))
        def _():
            out[:, (j % 2) * 256:(j % 2) * 256 + 256] = flat[j]

    @pl.when(x == 0)
    def _():
        for copy in u_scatter:
            copy.wait_send()

    @pl.when(t_source)
    def _():
        @pl.loop(1, RN)
        def _(d):
            t_copy((piece + d) % RN).wait_send()

    @pl.when(z < 4)
    def _():
        for copy in a_scatter:
            copy.wait_send()

    for home in range(4):
        @pl.when(z == home)
        def _():
            for copy in far[home]:
                copy.wait_send()

        @pl.when(z % 4 == home)
        def _():
            for copy in near[home]:
                copy.wait_send()


def on_device(front, child_updates, block_lists, pivot_inverses):
    vmem = pl.BlockSpec(memory_space=pltpu.VMEM)
    return pl.pallas_call(
        front_kernel,
        out_shape=jax.ShapeDtypeStruct((256, 512), F32),
        in_specs=[pl.BlockSpec(memory_space=pltpu.SMEM)] + [pl.BlockSpec(memory_space=pl.ANY)] * 3,
        out_specs=vmem,
        scratch_shapes=[
            pltpu.VMEM((256, 512), F32),
            pltpu.VMEM((8, 256, 256), F32),
            pltpu.VMEM((256, 512), F32),
            pltpu.VMEM((2, 4, 4, 64, 512), F32),
            pltpu.VMEM((2, 4, 4, 16, 8, 512), F32),
            pltpu.VMEM((16, 64, 512), F32),
            pltpu.VMEM((8, 128, 512), BF16),
            pltpu.VMEM((8, 128, 512), BF16),
            pltpu.VMEM((4, 256, 512), BF16),
            pltpu.VMEM((4, 256, 512), BF16),
            pltpu.VMEM((2048, 2048), BF16),
            pltpu.VMEM((2048, 2048), BF16),
            pltpu.VMEM((2048, 512), BF16),
            pltpu.VMEM((2048, 512), BF16),
            pltpu.VMEM((256, 2048), BF16),
            pltpu.VMEM((256, 2048), BF16),
            pltpu.VMEM((8, 256, 256), F32),
            pltpu.SemaphoreType.DMA((72,)),
            pltpu.SemaphoreType.DMA((72,)),
            pltpu.SemaphoreType.DMA((44,)),
            pltpu.SemaphoreType.DMA((44,)),
            pltpu.SemaphoreType.DMA((RN,)),
            pltpu.SemaphoreType.DMA((8,)),
            pltpu.SemaphoreType.DMA((8,)),
        ],
        compiler_params=pltpu.CompilerParams(
            collective_id=0, has_side_effects=True, vmem_limit_bytes=60 * 1024 * 1024),
    )(block_lists, front, child_updates, pivot_inverses)


def solution(mesh):
    return jax.shard_map(
        on_device,
        mesh=mesh,
        in_specs=(P("row", "col"), P("row", "col"), P(), P()),
        out_specs=P("row", "col"),
        check_vma=False,
    )
```

```python
import jax
import jax.numpy as jnp
from jax import lax
from jax.experimental import pallas as pl
from jax.experimental.pallas import tpu as pltpu
from jax.sharding import PartitionSpec as P

MESH = pl.DeviceIdType.MESH
F32 = jnp.float32
BF16 = jnp.bfloat16
ZN = 16
RN = 32


def start(copies):
    for copy in copies:
        copy.start()


def wait(copies):
    for copy in copies:
        copy.wait()


def parts(value):
    high = value.astype(BF16)
    return high, (value - high.astype(F32)).astype(BF16)


def product(ah, al, bh, bl):
    left = jnp.concatenate([ah, ah, al], axis=1)
    right = jnp.concatenate([bh, bl, bh], axis=0)
    return jnp.dot(left, right, preferred_element_type=F32)


def front_kernel(lists, front_hbm, child, pivots_hbm, out, front, pivots, own, u_buf, t_buf, a_buf, slab_low, slab_high, picked, routed,
                 wh, wl, xh, xl, mh, ml, flat, send, recv, z_send, z_recv, t_send, t_recv, local):
    r = lax.axis_index("row")
    z = lax.axis_index("col")
    x = r // 8
    y = (r // 2) % 4
    core = r % 2
    even = core == 0
    a1 = jnp.where(even, x, y)
    a2 = jnp.where(even, y, x)

    def at(px, py, pc):
        return (px * 8 + py * 2 + pc, z)

    sibling = at(x, y, 1 - core)

    def along_first(step):
        moved = (a1 + step) % 4
        return at(jnp.where(even, moved, x), jnp.where(even, y, moved), core)

    def along_second(step):
        moved = (a2 + step) % 4
        return at(jnp.where(even, x, moved), jnp.where(even, moved, y), core)

    front_in = pltpu.make_async_copy(front_hbm, front, local.at[5])
    pivots_in = pltpu.make_async_copy(pivots_hbm, pivots, local.at[6])
    front_in.start()
    pivots_in.start()

    group_z = (z // 4) * 4
    partners = [sibling]
    partners += [at((x + d) % 4, y, core) for d in (1, 2, 3)]
    partners += [at(x, (y + d) % 4, core) for d in (1, 2, 3)]
    partners += [(r, (z + d) % ZN) for d in (1, 4, 8, 12, 15)]
    partners += [(r, group_z + (z + d) % 4) for d in (1, 2, 3)]
    barrier = pltpu.get_barrier_semaphore()
    for partner in partners:
        pl.semaphore_signal(barrier, inc=1, device_id=partner, device_id_type=MESH)

    @pl.when(z < 4)
    def _():
        for k in range(8):
            @pl.when(r != k)
            def _():
                pl.semaphore_signal(barrier, inc=1, device_id=(k, z), device_id_type=MESH)

    pl.semaphore_wait(barrier, len(partners) + jnp.where((x == 0) & (z < 4), RN - 1, 0))

    used = [0]

    def to(src, dst, device):
        number = used[0]
        used[0] += 1
        return pltpu.make_async_remote_copy(
            src_ref=src, dst_ref=dst, send_sem=send.at[number], recv_sem=recv.at[number],
            device_id=device, device_id_type=MESH)

    def same(ref, device):
        return to(ref, ref, device)

    halves = [pl.ds(0, 128), pl.ds(128, 128)]
    slabs = [slab_low, slab_high]
    place_of = [((y + d) % 4) * 2 + core for d in range(4)]
    keep, first, passed = [], [], []
    for h, rows in enumerate(halves):
        slab = slabs[h]
        keep.append(pltpu.make_async_copy(child.at[rows], slab.at[place_of[0]], local.at[h]))
        first.append([to(child.at[rows], slab.at[place_of[0]], at(x, (y + d) % 4, core)) for d in (1, 3, 2)]
                     + [to(child.at[rows], slab.at[place_of[0]], sibling)])
        passed.append([same(slab.at[place_of[d]], sibling) for d in (1, 3, 2)])
    for h in range(2):
        start(first[h] + [keep[h]])

    group = x // 2
    base = (x % 2) * 8

    def choice(d):
        target = ((x + d) % 4) * 8 + y * 2 + core
        place = jnp.int32(0)
        found = jnp.int32(0)
        for m in range(8):
            hit = lists[group, base + m] == target
            place = jnp.where(hit, m, place)
            found = jnp.where(hit, 1, found)
        return place, found

    choices = [choice(d) for d in range(4)]
    up, opposite, down = [], [], []
    for h, rows in enumerate(halves):
        up.append(to(picked.at[1, rows], routed.at[1, rows], at((x + 1) % 4, y, core)))
        opposite.append(to(picked.at[2, rows], routed.at[2, rows], at((x + 2) % 4, y, core)))
        down.append(to(picked.at[3, rows], routed.at[3, rows], at((x + 3) % 4, y, core)))
    def pick(h, d):
        place, found = choices[d]

        @pl.loop(0, 4)
        def _(i):
            block = slabs[h][place, pl.ds(pl.multiple_of(i * 32, 32), 32), :].astype(F32)
            rows = pl.ds(pl.multiple_of(h * 128 + i * 32, 32), 32)
            picked[d, rows, :] = jnp.where(found > 0, block, 0.0).astype(BF16)

    for h in range(2):
        wait(first[h][:3])
        start(passed[h])
        keep[h].wait()
        first[h][3].wait()
        wait(passed[h])
        pick(h, 2)
        opposite[h].start()
    for h in range(2):
        pick(h, 1)
        pl.when(x < 2)(lambda: up[h].start())
        pick(h, 3)
        pl.when(x >= 2)(lambda: down[h].start())
        pick(h, 0)
    front_in.wait()
    for h in range(2):
        opposite[h].wait()

        @pl.loop(0, 4)
        def _(i):
            rows = pl.ds(pl.multiple_of(h * 128 + i * 32, 32), 32)
            own[rows, :] = front[rows, :] + picked[0, rows, :].astype(F32) + routed[2, rows, :].astype(F32)

    inner = (x == 1) | (x == 2)
    for h in range(2):
        pl.when(x < 2)(lambda: up[h].wait_send())
        pl.when(x >= 2)(lambda: down[h].wait_send())

        @pl.when(inner)
        def _():
            up[h].wait_recv()
            down[h].wait_recv()

            @pl.loop(0, 4)
            def _(i):
                rows = pl.ds(pl.multiple_of(h * 128 + i * 32, 32), 32)
                own[rows, :] = own[rows, :] + routed[1, rows, :].astype(F32) + routed[3, rows, :].astype(F32)

    def z_copy(src, dst, number, arrival, pz):
        return pltpu.make_async_remote_copy(
            src_ref=src, dst_ref=dst, send_sem=z_send.at[number], recv_sem=z_recv.at[arrival],
            device_id=(r, pz % ZN), device_id_type=MESH)

    def u_place(px):
        return u_buf.at[core, jnp.where(even, y, px), jnp.where(even, px, y)]

    u_scatter = [to(own.at[64 * q:64 * q + 64], u_place(q), at(q, y, core)) for q in (1, 2, 3)]
    u_keep = pltpu.make_async_copy(own.at[0:64], u_place(0), local.at[2])

    @pl.when(x == 0)
    def _():
        start(u_scatter)
        u_keep.start()

    row_block = y * 2 + core
    piece = core * 16 + a2 * 4 + a1
    t_slot = jnp.minimum(z * z + row_block, 15)

    def t_copy(p):
        pc, p2, p1 = p // 16, (p // 4) % 4, p % 4
        px, py = jnp.where(pc == 0, p1, p2), jnp.where(pc == 0, p2, p1)
        return pltpu.make_async_remote_copy(
            src_ref=own.at[pl.ds(pl.multiple_of(p * 8, 8), 8)], dst_ref=t_buf.at[pc, p2, p1, t_slot],
            send_sem=t_send.at[p], recv_sem=t_recv.at[row_block],
            device_id=at(px, py, pc), device_id_type=MESH)

    t_keep = pltpu.make_async_copy(
        own.at[pl.ds(pl.multiple_of(piece * 8, 8), 8)], t_buf.at[core, a2, a1, t_slot], local.at[3])
    t_source = (x == 0) & (z < 4) & (row_block <= 2 * z)

    @pl.when(t_source)
    def _():
        t_keep.start()

        @pl.loop(1, RN)
        def _(d):
            t_copy((piece + d) % RN).start()

    a_scatter = [z_copy(own.at[64 * q:64 * q + 64], a_buf.at[(z + 4 * q) % ZN], 8 + q, 8 + q, z + 4 * q)
                 for q in (1, 2, 3)]
    a_keep = pltpu.make_async_copy(own.at[0:64], a_buf.at[z], local.at[4])

    @pl.when(z < 4)
    def _():
        start(a_scatter)
        a_keep.start()

    def a_step(s, half):
        rows = slice(32 * half, 32 * half + 32)
        back, ahead = a_buf.at[(z + ZN - s) % ZN, rows], a_buf.at[(z + s) % ZN, rows]
        number = 12 + 4 * s + 2 * half
        pair = [z_copy(back, back, number, number, z + 1), z_copy(ahead, ahead, number + 1, number + 1, z + ZN - 1)]
        return pair if s < 7 else pair[half:half + 1]

    ring = [a_step(s, half) for s in range(8) for half in range(2)]
    turn = [0]

    def advance(count=1):
        for _ in range(count):
            event = turn[0]
            turn[0] += 1
            if event == 0:
                for q in (1, 2, 3):
                    pl.when(z // 4 == q)(lambda: a_scatter[q - 1].wait_recv())
                pl.when(z < 4)(lambda: a_keep.wait())
                start(ring[0] + ring[1])
            elif event <= 16:
                wait(ring[event - 1])
                if event + 1 < 16:
                    start(ring[event + 1])

    def plane_first(ref):
        return [same(ref(core, a2, a1), along_first(d)) for d in (1, 3, 2)]

    def plane_second(ref):
        return [same(ref(core, a2, slice(0, 4)), along_second(d)) for d in (1, 3)] + [
            same(ref(core, a2, slice(0, 4)), sibling)]

    def plane_third(ref):
        return [same(ref(core, (a2 + 3) % 4, slice(0, 2)), along_second(1)),
                same(ref(core, (a2 + 1) % 4, slice(2, 4)), along_second(3)),
                same(ref(core, (a2 + 3) % 4, slice(0, 4)), sibling),
                same(ref(core, (a2 + 1) % 4, slice(0, 4)), sibling)]

    def plane_last(ref):
        return [same(ref(core, (a2 + 2) % 4, slice(0, 4)), sibling)]

    def plane_gather(ref):
        return plane_first(ref), plane_second(ref), plane_third(ref), plane_last(ref)

    u_one, u_two, u_three, u_four = plane_gather(lambda *place: u_buf.at[place])
    for q in (1, 2, 3):
        pl.when(x == q)(lambda: u_scatter[q - 1].wait_recv())
    pl.when(x == 0)(lambda: u_keep.wait())
    start(u_one)

    for k in range(7):
        source_here = (x == 0) & (row_block == k)

        @pl.when((z < 4) & (2 * z >= k))
        def _():
            slot = jnp.minimum(z * z + k, 15)
            arrived = t_buf.at[core, a2, a1, slot]
            copy = pltpu.make_async_remote_copy(
                src_ref=arrived, dst_ref=arrived, send_sem=t_send.at[0], recv_sem=t_recv.at[k],
                device_id=sibling, device_id_type=MESH)
            pl.when(source_here)(lambda: t_keep.wait())
            pl.when(jnp.logical_not(source_here))(lambda: copy.wait_recv())

    homes = [t_buf.at[core, a2, a1, home * home:(home + 1) * (home + 1)] for home in range(4)]

    far = [[z_copy(homes[home], homes[home], d, home, z + 4 * d) for d in (1, 2, 3)] for home in range(4)]
    near = [[z_copy(homes[home], homes[home], 3 + d, 4 + home, group_z + (z + d) % 4) for d in (1, 2, 3)]
            for home in range(4)]
    for home in range(4):
        pl.when(z == home)(lambda: start(far[home]))

    wait(u_one)
    start(u_two)
    for home in range(4):
        pl.when((z >= 4) & (z % 4 == home))(lambda: far[home][0].wait_recv())
        pl.when(z % 4 == home)(lambda: start(near[home]))

    wide = plane_gather(lambda *place: t_buf.at[place + (slice(0, 9),)])
    narrow = plane_gather(lambda *place: t_buf.at[place + (slice(9, 16),)])
    advance()
    wait(u_two[:2])
    start(u_three)
    for home in range(3):
        pl.when(z % 4 != home)(lambda: near[home][0].wait_recv())
    start(wide[0])
    advance(2)
    wait(u_three[:2])
    start(u_four)
    wait(wide[0])
    start(wide[1])
    pl.when(z % 4 != 3)(lambda: near[3][0].wait_recv())
    start(narrow[0])
    advance(2)
    wait(u_two[2:] + u_three[2:] + u_four)
    wait(wide[1][:2])
    start(wide[2])
    wait(narrow[0])
    start(narrow[1])
    advance(2)
    wait(wide[2][:2])
    start(wide[3])
    advance(2)
    pivots_in.wait()
    wait(wide[1][2:] + wide[2][2:] + wide[3])

    columns = lax.broadcasted_iota(jnp.int32, (1, 512), 1) // 256 + 2 * z
    blocks = [pl.ds(256 * j, 256) for j in range(8)]

    def lead(j, c):
        n = 256 * j
        me, cols = blocks[j], pl.ds(512 * c, 512)
        value = t_buf[:, :, :, c * c + j].reshape(256, 512)
        if j:
            value = value - product(wh[me, 0:n], wl[me, 0:n], wh[0:n, cols], wl[0:n, cols])
        high, low = parts(value)
        wh[me, cols] = high
        wl[me, cols] = low
        pivot_high, pivot_low = parts(pivots[j])
        scaled = product(pivot_high, pivot_low, high, low)
        for half in range(2):
            i = 2 * c + half
            if i > j:
                wh[blocks[i], me], wl[blocks[i], me] = parts(scaled[:, half * 256:half * 256 + 256].T)

    def plane_row(j):
        n = 256 * j
        me = blocks[j]
        value = (u_buf[0, j // 2] if j % 2 == 0 else u_buf[1, :, j // 2]).reshape(256, 512)
        if j:
            value = value - product(wh[me, 0:n], wl[me, 0:n], xh[0:n], xl[0:n])
        xh[me], xl[me] = parts(jnp.where(columns > j, value, 0.0))

    def panel_step(j):
        n = 256 * j
        me = blocks[j]
        side = slice((j % 2) * 256, (j % 2) * 256 + 256)
        panel = jnp.concatenate([a_buf[4 * q + j // 2, :, side] for q in range(4)], axis=0)
        if j:
            panel = panel - product(mh[:, 0:n], ml[:, 0:n], wh[0:n, me], wl[0:n, me])
        high, low = parts(jnp.where(r > j, panel, 0.0))
        pivot_high, pivot_low = parts(pivots[j])
        flat[j] = product(high, low, pivot_high, pivot_low)
        mh[:, me], ml[:, me] = parts(flat[j])

    for j in range(6):
        for c in range((j + 1) // 2, 3):
            lead(j, c)
        if j == 0:
            wait(narrow[1][:2])
            start(narrow[2])
        plane_row(j)
        if j == 2:
            wait(narrow[2][:2])
            start(narrow[3])
        advance()
    wait(narrow[1][2:] + narrow[2][2:] + narrow[3])
    for j in range(7):
        lead(j, 3)
        if j % 2:
            advance()
    plane_row(6)
    plane_row(7)
    advance(17 - turn[0])
    for j in range(8):
        panel_step(j)
    out[...] = own[...] - product(mh[...], ml[...], xh[...], xl[...])
    for j in range(8):
        @pl.when((z == j // 2) & (r > j))
        def _():
            out[:, (j % 2) * 256:(j % 2) * 256 + 256] = flat[j]

    @pl.when(x == 0)
    def _():
        for copy in u_scatter:
            copy.wait_send()

    @pl.when(t_source)
    def _():
        @pl.loop(1, RN)
        def _(d):
            t_copy((piece + d) % RN).wait_send()

    @pl.when(z < 4)
    def _():
        for copy in a_scatter:
            copy.wait_send()

    for home in range(4):
        @pl.when(z == home)
        def _():
            for copy in far[home]:
                copy.wait_send()

        @pl.when(z % 4 == home)
        def _():
            for copy in near[home]:
                copy.wait_send()


def on_device(front, child_updates, block_lists, pivot_inverses):
    vmem = pl.BlockSpec(memory_space=pltpu.VMEM)
    return pl.pallas_call(
        front_kernel,
        out_shape=jax.ShapeDtypeStruct((256, 512), F32),
        in_specs=[pl.BlockSpec(memory_space=pltpu.SMEM)] + [pl.BlockSpec(memory_space=pl.ANY)] * 3,
        out_specs=vmem,
        scratch_shapes=[
            pltpu.VMEM((256, 512), F32),
            pltpu.VMEM((8, 256, 256), F32),
            pltpu.VMEM((256, 512), F32),
            pltpu.VMEM((2, 4, 4, 64, 512), F32),
            pltpu.VMEM((2, 4, 4, 16, 8, 512), F32),
            pltpu.VMEM((16, 64, 512), F32),
            pltpu.VMEM((8, 128, 512), BF16),
            pltpu.VMEM((8, 128, 512), BF16),
            pltpu.VMEM((4, 256, 512), BF16),
            pltpu.VMEM((4, 256, 512), BF16),
            pltpu.VMEM((2048, 2048), BF16),
            pltpu.VMEM((2048, 2048), BF16),
            pltpu.VMEM((2048, 512), BF16),
            pltpu.VMEM((2048, 512), BF16),
            pltpu.VMEM((256, 2048), BF16),
            pltpu.VMEM((256, 2048), BF16),
            pltpu.VMEM((8, 256, 256), F32),
            pltpu.SemaphoreType.DMA((72,)),
            pltpu.SemaphoreType.DMA((72,)),
            pltpu.SemaphoreType.DMA((44,)),
            pltpu.SemaphoreType.DMA((44,)),
            pltpu.SemaphoreType.DMA((RN,)),
            pltpu.SemaphoreType.DMA((8,)),
            pltpu.SemaphoreType.DMA((8,)),
        ],
        compiler_params=pltpu.CompilerParams(
            collective_id=0, has_side_effects=True, vmem_limit_bytes=60 * 1024 * 1024),
    )(block_lists, front, child_updates, pivot_inverses)


def solution(mesh):
    return jax.shard_map(
        on_device,
        mesh=mesh,
        in_specs=(P("row", "col"), P("row", "col"), P(), P()),
        out_specs=P("row", "col"),
        check_vma=False,
    )
```

```python
import jax
import jax.numpy as jnp
from jax import lax
from jax.experimental import pallas as pl
from jax.experimental.pallas import tpu as pltpu
from jax.sharding import PartitionSpec as P

MESH = pl.DeviceIdType.MESH
F32 = jnp.float32
BF16 = jnp.bfloat16
ZN = 16
RN = 32


def start(copies):
    for copy in copies:
        copy.start()


def wait(copies):
    for copy in copies:
        copy.wait()


def parts(value):
    high = value.astype(BF16)
    return high, (value - high.astype(F32)).astype(BF16)


def product(ah, al, bh, bl):
    left = jnp.concatenate([ah, ah, al], axis=1)
    right = jnp.concatenate([bh, bl, bh], axis=0)
    return jnp.dot(left, right, preferred_element_type=F32)


def front_kernel(lists, front_hbm, child, pivots_hbm, out, front, pivots, own, u_buf, t_buf, a_buf, slab_low, slab_high, picked, routed,
                 wh, wl, xh, xl, mh, ml, flat, send, recv, z_send, z_recv, t_send, t_recv, local):
    r = lax.axis_index("row")
    z = lax.axis_index("col")
    x = r // 8
    y = (r // 2) % 4
    core = r % 2
    even = core == 0
    a1 = jnp.where(even, x, y)
    a2 = jnp.where(even, y, x)

    def at(px, py, pc):
        return (px * 8 + py * 2 + pc, z)

    sibling = at(x, y, 1 - core)

    def along_first(step):
        moved = (a1 + step) % 4
        return at(jnp.where(even, moved, x), jnp.where(even, y, moved), core)

    def along_second(step):
        moved = (a2 + step) % 4
        return at(jnp.where(even, x, moved), jnp.where(even, moved, y), core)

    front_in = pltpu.make_async_copy(front_hbm, front, local.at[5])
    pivots_in = pltpu.make_async_copy(pivots_hbm, pivots, local.at[6])
    front_in.start()
    pivots_in.start()

    group_z = (z // 4) * 4
    partners = [sibling]
    partners += [at((x + d) % 4, y, core) for d in (1, 2, 3)]
    partners += [at(x, (y + d) % 4, core) for d in (1, 2, 3)]
    partners += [(r, (z + d) % ZN) for d in (1, 4, 8, 12, 15)]
    partners += [(r, group_z + (z + d) % 4) for d in (1, 2, 3)]
    barrier = pltpu.get_barrier_semaphore()
    for partner in partners:
        pl.semaphore_signal(barrier, inc=1, device_id=partner, device_id_type=MESH)

    @pl.when(z < 4)
    def _():
        for k in range(8):
            @pl.when(r != k)
            def _():
                pl.semaphore_signal(barrier, inc=1, device_id=(k, z), device_id_type=MESH)

    pl.semaphore_wait(barrier, len(partners) + jnp.where((x == 0) & (z < 4), RN - 1, 0))

    used = [0]

    def to(src, dst, device):
        number = used[0]
        used[0] += 1
        return pltpu.make_async_remote_copy(
            src_ref=src, dst_ref=dst, send_sem=send.at[number], recv_sem=recv.at[number],
            device_id=device, device_id_type=MESH)

    def same(ref, device):
        return to(ref, ref, device)

    halves = [pl.ds(0, 128), pl.ds(128, 128)]
    slabs = [slab_low, slab_high]
    place_of = [((y + d) % 4) * 2 + core for d in range(4)]
    keep, first, passed = [], [], []
    for h, rows in enumerate(halves):
        slab = slabs[h]
        keep.append(pltpu.make_async_copy(child.at[rows], slab.at[place_of[0]], local.at[h]))
        first.append([to(child.at[rows], slab.at[place_of[0]], at(x, (y + d) % 4, core)) for d in (1, 3, 2)]
                     + [to(child.at[rows], slab.at[place_of[0]], sibling)])
        passed.append([same(slab.at[place_of[d]], sibling) for d in (1, 3, 2)])
    for h in range(2):
        start(first[h] + [keep[h]])

    group = x // 2
    base = (x % 2) * 8

    def choice(d):
        target = ((x + d) % 4) * 8 + y * 2 + core
        place = jnp.int32(0)
        found = jnp.int32(0)
        for m in range(8):
            hit = lists[group, base + m] == target
            place = jnp.where(hit, m, place)
            found = jnp.where(hit, 1, found)
        return place, found

    choices = [choice(d) for d in range(4)]
    up, opposite, down = [], [], []
    for h, rows in enumerate(halves):
        up.append(to(picked.at[1, rows], routed.at[1, rows], at((x + 1) % 4, y, core)))
        opposite.append(to(picked.at[2, rows], routed.at[2, rows], at((x + 2) % 4, y, core)))
        down.append(to(picked.at[3, rows], routed.at[3, rows], at((x + 3) % 4, y, core)))
    def pick(h, d):
        place, found = choices[d]

        @pl.loop(0, 4)
        def _(i):
            block = slabs[h][place, pl.ds(pl.multiple_of(i * 32, 32), 32), :].astype(F32)
            rows = pl.ds(pl.multiple_of(h * 128 + i * 32, 32), 32)
            picked[d, rows, :] = jnp.where(found > 0, block, 0.0).astype(BF16)

    for h in range(2):
        wait(first[h][:3])
        start(passed[h])
        keep[h].wait()
        first[h][3].wait()
        wait(passed[h])
        pick(h, 2)
        opposite[h].start()
    for h in range(2):
        pick(h, 1)
        pl.when(x < 2)(lambda: up[h].start())
        pick(h, 3)
        pl.when(x >= 2)(lambda: down[h].start())
        pick(h, 0)
    front_in.wait()
    for h in range(2):
        opposite[h].wait()

        @pl.loop(0, 4)
        def _(i):
            rows = pl.ds(pl.multiple_of(h * 128 + i * 32, 32), 32)
            own[rows, :] = front[rows, :] + picked[0, rows, :].astype(F32) + routed[2, rows, :].astype(F32)

    inner = (x == 1) | (x == 2)
    for h in range(2):
        pl.when(x < 2)(lambda: up[h].wait_send())
        pl.when(x >= 2)(lambda: down[h].wait_send())

        @pl.when(inner)
        def _():
            up[h].wait_recv()
            down[h].wait_recv()

            @pl.loop(0, 4)
            def _(i):
                rows = pl.ds(pl.multiple_of(h * 128 + i * 32, 32), 32)
                own[rows, :] = own[rows, :] + routed[1, rows, :].astype(F32) + routed[3, rows, :].astype(F32)

    def z_copy(src, dst, number, arrival, pz):
        return pltpu.make_async_remote_copy(
            src_ref=src, dst_ref=dst, send_sem=z_send.at[number], recv_sem=z_recv.at[arrival],
            device_id=(r, pz % ZN), device_id_type=MESH)

    def u_place(px):
        return u_buf.at[core, jnp.where(even, y, px), jnp.where(even, px, y)]

    u_scatter = [to(own.at[64 * q:64 * q + 64], u_place(q), at(q, y, core)) for q in (1, 2, 3)]
    u_keep = pltpu.make_async_copy(own.at[0:64], u_place(0), local.at[2])

    @pl.when(x == 0)
    def _():
        start(u_scatter)
        u_keep.start()

    row_block = y * 2 + core
    piece = core * 16 + a2 * 4 + a1
    t_slot = jnp.minimum(z * z + row_block, 15)

    def t_copy(p):
        pc, p2, p1 = p // 16, (p // 4) % 4, p % 4
        px, py = jnp.where(pc == 0, p1, p2), jnp.where(pc == 0, p2, p1)
        return pltpu.make_async_remote_copy(
            src_ref=own.at[pl.ds(pl.multiple_of(p * 8, 8), 8)], dst_ref=t_buf.at[pc, p2, p1, t_slot],
            send_sem=t_send.at[p], recv_sem=t_recv.at[row_block],
            device_id=at(px, py, pc), device_id_type=MESH)

    t_keep = pltpu.make_async_copy(
        own.at[pl.ds(pl.multiple_of(piece * 8, 8), 8)], t_buf.at[core, a2, a1, t_slot], local.at[3])
    t_source = (x == 0) & (z < 4) & (row_block <= 2 * z)

    @pl.when(t_source)
    def _():
        t_keep.start()

        @pl.loop(1, RN)
        def _(d):
            t_copy((piece + d) % RN).start()

    a_scatter = [z_copy(own.at[64 * q:64 * q + 64], a_buf.at[(z + 4 * q) % ZN], 8 + q, 8 + q, z + 4 * q)
                 for q in (1, 2, 3)]
    a_keep = pltpu.make_async_copy(own.at[0:64], a_buf.at[z], local.at[4])

    @pl.when(z < 4)
    def _():
        start(a_scatter)
        a_keep.start()

    def a_step(s, half):
        rows = slice(32 * half, 32 * half + 32)
        back, ahead = a_buf.at[(z + ZN - s) % ZN, rows], a_buf.at[(z + s) % ZN, rows]
        number = 12 + 4 * s + 2 * half
        pair = [z_copy(back, back, number, number, z + 1), z_copy(ahead, ahead, number + 1, number + 1, z + ZN - 1)]
        return pair if s < 7 else pair[half:half + 1]

    ring = [a_step(s, half) for s in range(8) for half in range(2)]
    turn = [0]

    def advance(count=1):
        for _ in range(count):
            event = turn[0]
            turn[0] += 1
            if event == 0:
                for q in (1, 2, 3):
                    pl.when(z // 4 == q)(lambda: a_scatter[q - 1].wait_recv())
                pl.when(z < 4)(lambda: a_keep.wait())
                start(ring[0] + ring[1])
            elif event <= 16:
                wait(ring[event - 1])
                if event + 1 < 16:
                    start(ring[event + 1])

    def plane_first(ref):
        return [same(ref(core, a2, a1), along_first(d)) for d in (1, 3, 2)]

    def plane_second(ref):
        return [same(ref(core, a2, slice(0, 4)), along_second(d)) for d in (1, 3)] + [
            same(ref(core, a2, slice(0, 4)), sibling)]

    def plane_third(ref):
        return [same(ref(core, (a2 + 3) % 4, slice(0, 2)), along_second(1)),
                same(ref(core, (a2 + 1) % 4, slice(2, 4)), along_second(3)),
                same(ref(core, (a2 + 3) % 4, slice(0, 4)), sibling),
                same(ref(core, (a2 + 1) % 4, slice(0, 4)), sibling)]

    def plane_last(ref):
        return [same(ref(core, (a2 + 2) % 4, slice(0, 4)), sibling)]

    def plane_gather(ref):
        return plane_first(ref), plane_second(ref), plane_third(ref), plane_last(ref)

    u_one, u_two, u_three, u_four = plane_gather(lambda *place: u_buf.at[place])
    for q in (1, 2, 3):
        pl.when(x == q)(lambda: u_scatter[q - 1].wait_recv())
    pl.when(x == 0)(lambda: u_keep.wait())
    start(u_one)

    for k in range(7):
        source_here = (x == 0) & (row_block == k)

        @pl.when((z < 4) & (2 * z >= k))
        def _():
            slot = jnp.minimum(z * z + k, 15)
            arrived = t_buf.at[core, a2, a1, slot]
            copy = pltpu.make_async_remote_copy(
                src_ref=arrived, dst_ref=arrived, send_sem=t_send.at[0], recv_sem=t_recv.at[k],
                device_id=sibling, device_id_type=MESH)
            pl.when(source_here)(lambda: t_keep.wait())
            pl.when(jnp.logical_not(source_here))(lambda: copy.wait_recv())

    homes = [t_buf.at[core, a2, a1, home * home:(home + 1) * (home + 1)] for home in range(4)]

    far = [[z_copy(homes[home], homes[home], d, home, z + 4 * d) for d in (1, 2, 3)] for home in range(4)]
    near = [[z_copy(homes[home], homes[home], 3 + d, 4 + home, group_z + (z + d) % 4) for d in (1, 2, 3)]
            for home in range(4)]
    for home in range(4):
        pl.when(z == home)(lambda: start(far[home]))

    wait(u_one)
    start(u_two)
    for home in range(4):
        pl.when((z >= 4) & (z % 4 == home))(lambda: far[home][0].wait_recv())
        pl.when(z % 4 == home)(lambda: start(near[home]))

    wide = plane_gather(lambda *place: t_buf.at[place + (slice(0, 9),)])
    narrow = plane_gather(lambda *place: t_buf.at[place + (slice(9, 16),)])
    advance()
    wait(u_two[:2])
    start(u_three)
    for home in range(3):
        pl.when(z % 4 != home)(lambda: near[home][0].wait_recv())
    start(wide[0])
    advance(2)
    wait(u_three[:2])
    start(u_four)
    wait(wide[0])
    start(wide[1])
    pl.when(z % 4 != 3)(lambda: near[3][0].wait_recv())
    start(narrow[0])
    advance(2)
    wait(u_two[2:] + u_three[2:] + u_four)
    wait(wide[1][:2])
    start(wide[2])
    wait(narrow[0])
    start(narrow[1])
    advance(2)
    wait(wide[2][:2])
    start(wide[3])
    advance(2)
    pivots_in.wait()
    wait(wide[1][2:] + wide[2][2:] + wide[3])

    columns = lax.broadcasted_iota(jnp.int32, (1, 512), 1) // 256 + 2 * z
    blocks = [pl.ds(256 * j, 256) for j in range(8)]

    def lead(j, c):
        n = 256 * j
        me, cols = blocks[j], pl.ds(512 * c, 512)
        value = t_buf[:, :, :, c * c + j].reshape(256, 512)
        if j:
            value = value - product(wh[me, 0:n], wl[me, 0:n], wh[0:n, cols], wl[0:n, cols])
        high, low = parts(value)
        wh[me, cols] = high
        wl[me, cols] = low
        pivot_high, pivot_low = parts(pivots[j])
        scaled = product(pivot_high, pivot_low, high, low)
        for half in range(2):
            i = 2 * c + half
            if i > j:
                wh[blocks[i], me], wl[blocks[i], me] = parts(scaled[:, half * 256:half * 256 + 256].T)

    def plane_row(j):
        n = 256 * j
        me = blocks[j]
        value = (u_buf[0, j // 2] if j % 2 == 0 else u_buf[1, :, j // 2]).reshape(256, 512)
        if j:
            value = value - product(wh[me, 0:n], wl[me, 0:n], xh[0:n], xl[0:n])
        xh[me], xl[me] = parts(jnp.where(columns > j, value, 0.0))

    def panel_step(j):
        n = 256 * j
        me = blocks[j]
        side = slice((j % 2) * 256, (j % 2) * 256 + 256)
        panel = jnp.concatenate([a_buf[4 * q + j // 2, :, side] for q in range(4)], axis=0)
        if j:
            panel = panel - product(mh[:, 0:n], ml[:, 0:n], wh[0:n, me], wl[0:n, me])
        high, low = parts(jnp.where(r > j, panel, 0.0))
        pivot_high, pivot_low = parts(pivots[j])
        flat[j] = product(high, low, pivot_high, pivot_low)
        mh[:, me], ml[:, me] = parts(flat[j])

    for j in range(6):
        for c in range((j + 1) // 2, 3):
            lead(j, c)
        if j == 0:
            wait(narrow[1][:2])
            start(narrow[2])
        plane_row(j)
        if j == 2:
            wait(narrow[2][:2])
            start(narrow[3])
        advance()
    wait(narrow[1][2:] + narrow[2][2:] + narrow[3])
    for j in range(4):
        lead(j, 3)
        if j % 2:
            advance()
    advance(17 - turn[0])
    panel_step(0)
    for j in (4, 5, 6):
        lead(j, 3)
        panel_step(2 * j - 7)
        panel_step(2 * j - 6) if j < 6 else plane_row(6)
    panel_step(6)
    plane_row(7)
    panel_step(7)
    out[...] = own[...] - product(mh[...], ml[...], xh[...], xl[...])
    for j in range(8):
        @pl.when((z == j // 2) & (r > j))
        def _():
            out[:, (j % 2) * 256:(j % 2) * 256 + 256] = flat[j]

    @pl.when(x == 0)
    def _():
        for copy in u_scatter:
            copy.wait_send()

    @pl.when(t_source)
    def _():
        @pl.loop(1, RN)
        def _(d):
            t_copy((piece + d) % RN).wait_send()

    @pl.when(z < 4)
    def _():
        for copy in a_scatter:
            copy.wait_send()

    for home in range(4):
        @pl.when(z == home)
        def _():
            for copy in far[home]:
                copy.wait_send()

        @pl.when(z % 4 == home)
        def _():
            for copy in near[home]:
                copy.wait_send()


def on_device(front, child_updates, block_lists, pivot_inverses):
    vmem = pl.BlockSpec(memory_space=pltpu.VMEM)
    return pl.pallas_call(
        front_kernel,
        out_shape=jax.ShapeDtypeStruct((256, 512), F32),
        in_specs=[pl.BlockSpec(memory_space=pltpu.SMEM)] + [pl.BlockSpec(memory_space=pl.ANY)] * 3,
        out_specs=vmem,
        scratch_shapes=[
            pltpu.VMEM((256, 512), F32),
            pltpu.VMEM((8, 256, 256), F32),
            pltpu.VMEM((256, 512), F32),
            pltpu.VMEM((2, 4, 4, 64, 512), F32),
            pltpu.VMEM((2, 4, 4, 16, 8, 512), F32),
            pltpu.VMEM((16, 64, 512), F32),
            pltpu.VMEM((8, 128, 512), BF16),
            pltpu.VMEM((8, 128, 512), BF16),
            pltpu.VMEM((4, 256, 512), BF16),
            pltpu.VMEM((4, 256, 512), BF16),
            pltpu.VMEM((2048, 2048), BF16),
            pltpu.VMEM((2048, 2048), BF16),
            pltpu.VMEM((2048, 512), BF16),
            pltpu.VMEM((2048, 512), BF16),
            pltpu.VMEM((256, 2048), BF16),
            pltpu.VMEM((256, 2048), BF16),
            pltpu.VMEM((8, 256, 256), F32),
            pltpu.SemaphoreType.DMA((72,)),
            pltpu.SemaphoreType.DMA((72,)),
            pltpu.SemaphoreType.DMA((44,)),
            pltpu.SemaphoreType.DMA((44,)),
            pltpu.SemaphoreType.DMA((RN,)),
            pltpu.SemaphoreType.DMA((8,)),
            pltpu.SemaphoreType.DMA((8,)),
        ],
        compiler_params=pltpu.CompilerParams(
            collective_id=0, has_side_effects=True, vmem_limit_bytes=60 * 1024 * 1024),
    )(block_lists, front, child_updates, pivot_inverses)


def solution(mesh):
    return jax.shard_map(
        on_device,
        mesh=mesh,
        in_specs=(P("row", "col"), P("row", "col"), P(), P()),
        out_specs=P("row", "col"),
        check_vma=False,
    )
```
